256 devices in a mesh: rows: 64 (over x, z, core), cols: 4 (over y).
Axes of the slice: x: 4, y: 4, z: 8, core: 2. Of those that a mesh axis runs over, the one named last changes fastest.
Arguments:
- embeddings: float32 [131072, 128], P('rows'), may hold values from -8 to 8
- centres: float32 [8192, 128], P('cols'), may hold values from -24 to 24
Outputs:
- new_centres: float32 [8192, 128], P('cols')
- expected_similarity: float32 [131072], P('rows')
The draws below stay inside these ranges and needn't reach their ends.
All inputs are finite; a program needn't handle non-finite values.
Results may differ from the reference program's by a relative error of at most 0.0003.
Values sent between devices are 32-bit elements; how exact they have to be, the bound alone decides.
A program may use at most 128 MiB of HBM per device.

```python
import jax
import jax.numpy as jnp
from jax import lax

EMB = 128
CLUSTERS = 8192
ITERS = 3
ROWS_DEV = 2048
MOLS = 131072
CLU_DEV = 2048


def draw_embeddings(key, part):
    key = jax.random.fold_in(key, 11)
    noise_key, dir_key, power_key = jax.random.split(key, 3)
    block_count = MOLS // ROWS_DEV
    directions = jnp.clip(jax.random.normal(dir_key, (block_count, EMB), jnp.float32), -6.0, 6.0)
    noise = jnp.clip(jax.random.normal(noise_key, (block_count, ROWS_DEV, EMB), jnp.float32), -6.0, 6.0)
    strength = jax.random.uniform(power_key, (block_count,), jnp.float32, 2.0, 3.0)
    shared = strength[:, None] * directions
    values = noise + shared[:, None, :]
    return jnp.clip(values, -8.0, 8.0).reshape(MOLS, EMB)


def draw_centres(key, part):
    key = jax.random.fold_in(key, 7)
    noise_key, dir_key = jax.random.split(key)
    block_count = CLUSTERS // CLU_DEV
    directions = jnp.clip(jax.random.normal(dir_key, (block_count, EMB), jnp.float32), -6.0, 6.0)
    block_of = jnp.arange(CLUSTERS) // CLU_DEV
    onehot = (block_of[:, None] == jnp.arange(block_count)[None, :]).astype(jnp.float32)
    level = jnp.arange(block_count).astype(jnp.float32)
    noise = jnp.clip(jax.random.normal(noise_key, (CLUSTERS, EMB), jnp.float32), -6.0, 6.0)
    strength = 1.0 + 0.5 * level
    shared = jnp.sum(onehot[:, :, None] * (strength[:, None] * directions)[None, :, :], axis=1)
    return noise + shared


def setup_inputs(seed: int = 0) -> dict:
    key_of = jax.random.split(jax.random.key(seed), 3)
    return {
        "embeddings": draw_embeddings(jax.random.fold_in(key_of[2], 71), 0),
        "centres": draw_centres(jax.random.fold_in(key_of[2], 71), 0),
    }


inverse_temp = 20.0

def unit_rows(value):
    return value * lax.rsqrt(lax.optimization_barrier(jnp.sum(value * value, axis=-1, keepdims=True)) + 1e-06)

def scores_of(block, unit_c):
    return jnp.dot(block, unit_c.T, precision=lax.Precision.HIGHEST, preferred_element_type=jnp.float32)

def reference(embeddings, centres):
    unit_x = unit_rows(embeddings)
    unit_c = unit_rows(centres)
    blocks = unit_x.reshape(MOLS // ROWS_DEV, ROWS_DEV, EMB)

    def expo_block(block):
        return jnp.exp(scores_of(block, unit_c) * inverse_temp)
    expo = lax.map(expo_block, blocks).reshape(MOLS, CLUSTERS)
    row_scale = jnp.ones((MOLS,), jnp.float32)
    for step in range(ITERS):
        col_scale = 1.0 / CLUSTERS / jnp.dot(row_scale, expo, precision=lax.Precision.HIGHEST)
        row_sum = jnp.dot(expo, col_scale, precision=lax.Precision.HIGHEST)
        row_scale = 1.0 / MOLS / row_sum

    def numer_block(block):
        scores = scores_of(block, unit_c)
        return jnp.dot(jnp.exp(scores * inverse_temp) * scores, col_scale, precision=lax.Precision.HIGHEST)
    numer = lax.map(numer_block, blocks).reshape(MOLS)
    expected = numer / row_sum
    inv_rows = (1.0 / row_sum).reshape(MOLS // ROWS_DEV, ROWS_DEV)

    def centre_step(total, pair):
        block, inv_block = pair
        tile = jnp.exp(scores_of(block, unit_c) * inverse_temp)
        weights = tile * col_scale[None, :] * inv_block[:, None]
        return (total + jnp.dot(weights.T, block, precision=lax.Precision.HIGHEST, preferred_element_type=jnp.float32), None)
    total, unused = lax.scan(centre_step, jnp.zeros((CLUSTERS, EMB), jnp.float32), (blocks, inv_rows))
    return (unit_rows(total), expected)
```

```python
import functools

import jax
import jax.numpy as jnp
from jax import lax
from jax.experimental import pallas as pl
from jax.experimental.pallas import tpu as pltpu
from jax.sharding import PartitionSpec as P

ITERS = 3
INV_TEMP = 20.0
EPS = 1e-06
F32 = jnp.float32
BF16 = jnp.bfloat16
MESH = pl.DeviceIdType.MESH
CHIPS_X, CHIPS_Z, CHIPS_Y = 4, 8, 4


def split(value):
    hi = value.astype(BF16)
    lo = (value - hi.astype(F32)).astype(BF16)
    return hi, lo


def unit_rows(value):
    return value * lax.rsqrt(jnp.sum(value * value, axis=-1, keepdims=True) + EPS)


def to_sublanes(row, width=128):
    return jnp.broadcast_to(row, (width, 128)).T


def kernel(dims, mol_count, clu_count, x_ref, c_ref, out_ref, sim_ref, e_ref, t_ref, cc_ref, xc_ref, xu_ref,
           acc_ref, csb_ref, a_buf, z_buf, y_buf, l_buf, part_ref, core_buf, xr_buf, zs_buf, zr_buf,
           a_sem, z_sem, y_sem, l_sem, core_sem, xr_sem, zr_sem, gz_sem, gx_sem, gc_sem):
    nx, nz, ny = dims
    na = 2 * nx
    mols, clus = x_ref.shape[0], c_ref.shape[0]
    rows, y = lax.axis_index("rows"), lax.axis_index("cols")
    core = lax.rem(rows, 2)
    z = lax.rem(lax.div(rows, 2), nz)
    x = lax.div(rows, 2 * nz)
    a = x * 2 + core
    other = 1 - core

    def dev(x_at, z_at, core_at):
        return ((x_at * nz + z_at) * 2 + core_at, y)

    def dev_a(k):
        return dev(lax.div(k, 2), z, lax.rem(k, 2))

    def dev_z(k):
        return dev(x, k, core)

    def dev_x(k):
        return dev(k, z, core)

    def dev_y(k):
        return (rows, k)

    barrier = pltpu.get_barrier_semaphore()
    for me, n, at in ((a, na, dev_a), (z, nz, dev_z), (y, ny, dev_y)):
        for d in range(1, n):
            pl.semaphore_signal(barrier, inc=1, device_id=at(lax.rem(me + d, n)), device_id_type=MESH)

    step_p = min(256, mols)

    def prep(i, _):
        r = pl.ds(pl.multiple_of(i * step_p, step_p), step_p)
        hi, lo = split(unit_rows(c_ref[r, :]) * INV_TEMP)
        cc_ref[r, :] = jnp.concatenate([hi, lo, hi, lo], axis=1)
        u = unit_rows(x_ref[r, :])
        xu_ref[r, :] = u
        hi, lo = split(u)
        xc_ref[r, :] = jnp.concatenate([hi, hi, lo, lo], axis=1)
        return 0

    lax.fori_loop(0, mols // step_p, prep, 0)

    row_b, col_b = min(512, clus), min(512, mols)

    def score(i, _):
        r = pl.ds(pl.multiple_of(i * row_b, row_b), row_b)
        total = None
        for j in range(mols // col_b):
            m = pl.ds(j * col_b, col_b)
            t = lax.dot_general(cc_ref[r, :], xc_ref[m, :], (((1,), (1,)), ((), ())), preferred_element_type=F32)
            e = jnp.exp(t)
            t_ref[r, m] = t
            e_ref[r, m] = e
            part = e[:, 0:128]
            for k in range(1, col_b // 128):
                part = part + e[:, 128 * k:128 * (k + 1)]
            total = part if total is None else total + part
        acc_ref[r, :] = total
        return 0

    lax.fori_loop(0, clus // row_b, score, 0)

    pl.semaphore_wait(barrier, na + nz + ny - 3)

    sends = []

    def exchange(buf, sem, it, me, n, at):
        for d in range(1, n):
            k = lax.rem(me + d, n)
            copy = pltpu.make_async_remote_copy(
                src_ref=buf.at[it, me], dst_ref=buf.at[it, me], send_sem=sem.at[0, it, k], recv_sem=sem.at[1, it, me],
                device_id=at(k), device_id_type=MESH)
            copy.start()
            sends.append(copy)
        for d in range(1, n):
            k = lax.rem(me + n - d, n)
            pltpu.make_async_remote_copy(
                src_ref=buf.at[it, k], dst_ref=buf.at[it, k], send_sem=sem.at[0, it, k], recv_sem=sem.at[1, it, k],
                device_id=at(k), device_id_type=MESH).wait_recv()
        total = buf[it, 0]
        for k in range(1, n):
            total = total + buf[it, k]
        return total

    step_r = min(64, clus)

    for it in range(ITERS):
        if it > 0:
            scale = jnp.broadcast_to(1.0 / mol_count / row_sum, (8, mols))

            def col_pass(i, scale):
                for g in range(step_r // 8):
                    r = pl.ds(pl.multiple_of(i * step_r + g * 8, 8), 8)
                    p = e_ref[r, :] * scale
                    s = p[:, 0:128]
                    for k in range(1, mols // 128):
                        s = s + p[:, 128 * k:128 * (k + 1)]
                    acc_ref[r, :] = s
                return scale

            lax.fori_loop(0, clus // step_r, col_pass, scale)
        for j in range(clus // 128):
            s = slice(128 * j, 128 * (j + 1))
            a_buf[it, a, :, s] = jnp.sum(acc_ref[s, :].T, axis=0, keepdims=True)
        z_buf[it, z] = exchange(a_buf, a_sem, it, a, na, dev_a)
        col_mass = exchange(z_buf, z_sem, it, z, nz, dev_z)
        col_scale = 1.0 / clu_count / col_mass
        for j in range(clus // 128):
            s = slice(128 * j, 128 * (j + 1))
            csb_ref[s, :] = to_sublanes(col_scale[:, s])

        last = it == ITERS - 1

        def row_pass(i, carry):
            acc, num = carry
            for g in range(step_r // 8):
                r = pl.ds(pl.multiple_of(i * step_r + g * 8, 8), 8)
                w = e_ref[r, :] * jnp.concatenate([csb_ref[r, :]] * (mols // 128), axis=1)
                acc = acc + w
                if last:
                    num = num + w * t_ref[r, :]
            return acc, num

        zero = jnp.zeros((8, mols), F32)
        acc, num = lax.fori_loop(0, clus // step_r, row_pass, (zero, zero if last else jnp.zeros((8, 128), F32)))
        row_part = jnp.sum(acc, axis=0, keepdims=True)
        if last:
            l_buf[0, y, 0:1, :] = row_part
            l_buf[0, y, 1:2, :] = jnp.sum(num, axis=0, keepdims=True)
            both = exchange(l_buf, l_sem, 0, y, ny, dev_y)
            row_sum, numer = both[0:1, :], both[1:2, :]
        else:
            y_buf[it, y] = row_part
            row_sum = exchange(y_buf, y_sem, it, y, ny, dev_y)

    sim_ref[...] = numer / row_sum * (1.0 / INV_TEMP)

    inv = 1.0 / row_sum
    for j in range(mols // 128):
        s = slice(128 * j, 128 * (j + 1))
        hi, lo = split(xu_ref[s, :] * to_sublanes(inv[:, s]))
        xc_ref[s, 0:256] = jnp.concatenate([hi, lo], axis=1)

    blk = clus // na
    sub = blk // nz

    def block_rows(b):
        return pl.ds(pl.multiple_of(b * blk, blk), blk)

    def sums(b):
        r = block_rows(b)
        hi, lo = split(e_ref[r, :])
        p = jnp.dot(jnp.concatenate([hi, lo], axis=0), xc_ref[:, 0:256], preferred_element_type=F32)
        p = p[:, 0:128] + p[:, 128:256]
        return (p[0:blk] + p[blk:2 * blk]) * csb_ref[r, :]

    def remote(src, dst, send, recv, to):
        return pltpu.make_async_remote_copy(
            src_ref=src, dst_ref=dst, send_sem=send, recv_sem=recv, device_id=to, device_id_type=MESH)

    def to_core(q):
        b = other * nx + lax.rem(x + 1 + q, nx)
        return remote(part_ref.at[block_rows(b)], core_buf.at[q], core_sem.at[0, q], core_sem.at[1, q],
                      dev(x, z, other))

    def to_x(q):
        j = lax.rem(x + 1 + q, nx)
        return remote(part_ref.at[block_rows(core * nx + j)], xr_buf.at[x], xr_sem.at[0, j], xr_sem.at[1, x],
                      dev_x(j))

    def other_half(q, _):
        b = other * nx + lax.rem(x + 1 + q, nx)
        part_ref[block_rows(b), :] = sums(b)
        to_core(q).start()
        return 0

    lax.fori_loop(0, nx, other_half, 0)

    def own_half(q, _):
        j = lax.rem(x + 1 + q, nx)
        b = core * nx + j
        v = sums(b)
        to_core(q).wait_recv()
        v = v + core_buf[q]

        @pl.when(q < nx - 1)
        def _():
            part_ref[block_rows(b), :] = v
            to_x(q).start()

        @pl.when(q == nx - 1)
        def _():
            xr_buf[x] = v

        return 0

    lax.fori_loop(0, nx, own_half, 0)
    for d in range(1, nx):
        k = lax.rem(x + d, nx)
        remote(xr_buf.at[k], xr_buf.at[k], xr_sem.at[0, k], xr_sem.at[1, k], dev_x(k)).wait_recv()
    total = xr_buf[0]
    for k in range(1, nx):
        total = total + xr_buf[k]
    zs_buf[...] = total

    def sub_rows(k):
        return pl.ds(pl.multiple_of(k * sub, sub), sub)

    for d in range(1, nz):
        k = lax.rem(z + d, nz)
        copy = remote(zs_buf.at[sub_rows(k)], zr_buf.at[z], zr_sem.at[0, k], zr_sem.at[1, z], dev_z(k))
        copy.start()
        sends.append(copy)
    zr_buf[z] = zs_buf[sub_rows(z), :]
    for d in range(1, nz):
        k = lax.rem(z + nz - d, nz)
        remote(zr_buf.at[k], zr_buf.at[k], zr_sem.at[0, k], zr_sem.at[1, k], dev_z(k)).wait_recv()
    total = zr_buf[0]
    for k in range(1, nz):
        total = total + zr_buf[k]

    mine = core * nx + x

    def out_sub(k):
        return out_ref.at[pl.ds(pl.multiple_of(mine * blk + k * sub, sub), sub)]

    out_ref[pl.ds(pl.multiple_of(mine * blk + z * sub, sub), sub), :] = unit_rows(total)
    for d in range(1, nz):
        k = lax.rem(z + d, nz)
        copy = remote(out_sub(z), out_sub(z), gz_sem.at[0, k], gz_sem.at[1, z], dev_z(k))
        copy.start()
        sends.append(copy)
    for d in range(1, nz):
        k = lax.rem(z + nz - d, nz)
        remote(out_sub(k), out_sub(k), gz_sem.at[0, k], gz_sem.at[1, k], dev_z(k)).wait_recv()

    def out_blk(b):
        return out_ref.at[block_rows(b)]

    def forward(k):
        copy = remote(out_blk(core * nx + k), out_blk(core * nx + k), gc_sem.at[0, k], gc_sem.at[1, k],
                      dev(x, z, other))
        copy.start()
        sends.append(copy)

    for d in range(1, nx):
        k = lax.rem(x + d, nx)
        copy = remote(out_blk(mine), out_blk(mine), gx_sem.at[0, k], gx_sem.at[1, x], dev_x(k))
        copy.start()
        sends.append(copy)
    forward(x)
    for d in (1, 3, 2) if nx == 4 else range(1, nx):
        k = lax.rem(x + d, nx)
        remote(out_blk(core * nx + k), out_blk(core * nx + k), gx_sem.at[0, k], gx_sem.at[1, k],
               dev_x(k)).wait_recv()
        forward(k)
    for k in range(nx):
        b = other * nx + k
        remote(out_blk(b), out_blk(b), gc_sem.at[0, k], gc_sem.at[1, k], dev(x, z, other)).wait_recv()
    for copy in sends:
        copy.wait_send()
    for q in range(nx):
        to_core(q).wait_send()
        if q < nx - 1:
            to_x(q).wait_send()


def local(dims, embeddings, centres):
    nx, nz, ny = dims
    na = 2 * nx
    mols, emb = embeddings.shape
    clus = centres.shape[0]
    blk = clus // na
    sub = blk // nz
    dma = pltpu.SemaphoreType.DMA
    new_centres, expected = pl.pallas_call(
        functools.partial(kernel, dims, mols * lax.axis_size("rows"), clus * lax.axis_size("cols")),
        out_shape=(jax.ShapeDtypeStruct((clus, emb), F32), jax.ShapeDtypeStruct((1, mols), F32)),
        in_specs=[pl.BlockSpec(memory_space=pltpu.VMEM)] * 2,
        out_specs=(pl.BlockSpec(memory_space=pltpu.VMEM),) * 2,
        scratch_shapes=[
            pltpu.VMEM((clus, mols), F32),
            pltpu.VMEM((clus, mols), F32),
            pltpu.VMEM((clus, 4 * emb), BF16),
            pltpu.VMEM((mols, 4 * emb), BF16),
            pltpu.VMEM((mols, emb), F32),
            pltpu.VMEM((clus, 128), F32),
            pltpu.VMEM((clus, 128), F32),
            pltpu.VMEM((ITERS, na, 1, clus), F32),
            pltpu.VMEM((ITERS, nz, 1, clus), F32),
            pltpu.VMEM((ITERS - 1, ny, 1, mols), F32),
            pltpu.VMEM((1, ny, 2, mols), F32),
            pltpu.VMEM((clus, emb), F32),
            pltpu.VMEM((nx, blk, emb), F32),
            pltpu.VMEM((nx, blk, emb), F32),
            pltpu.VMEM((blk, emb), F32),
            pltpu.VMEM((nz, sub, emb), F32),
            dma((2, ITERS, na)),
            dma((2, ITERS, nz)),
            dma((2, ITERS - 1, ny)),
            dma((2, 1, ny)),
            dma((2, nx)),
            dma((2, nx)),
            dma((2, nz)),
            dma((2, nz)),
            dma((2, nx)),
            dma((2, nx)),
        ],
        compiler_params=pltpu.CompilerParams(
            collective_id=0, has_side_effects=True, vmem_limit_bytes=60 * 1024 * 1024),
        cost_estimate=pl.CostEstimate(flops=2 * 8 * mols * clus * emb, bytes_accessed=4 * 1024 * 1024,
                                      transcendentals=mols * clus),
    )(embeddings, centres)
    return new_centres, expected.reshape(mols)


def solution(mesh, dims=(CHIPS_X, CHIPS_Z, CHIPS_Y)):
    return jax.shard_map(
        functools.partial(local, dims), mesh=mesh, in_specs=(P("rows", None), P("cols", None)),
        out_specs=(P("cols", None), P("rows")), check_vma=False)
```

```python
import functools

import jax
import jax.numpy as jnp
from jax import lax
from jax.experimental import pallas as pl
from jax.experimental.pallas import tpu as pltpu
from jax.sharding import PartitionSpec as P

ITERS = 3
INV_TEMP = 20.0
EPS = 1e-06
F32 = jnp.float32
BF16 = jnp.bfloat16
MESH = pl.DeviceIdType.MESH
CHIPS_X, CHIPS_Z, CHIPS_Y = 4, 8, 4
CHUNKS = 4


def split(value):
    hi = value.astype(BF16)
    lo = (value - hi.astype(F32)).astype(BF16)
    return hi, lo


def unit_rows(value):
    return value * lax.rsqrt(jnp.sum(value * value, axis=-1, keepdims=True) + EPS)


def to_sublanes(row, width=128):
    return jnp.broadcast_to(row, (width, 128)).T


def kernel(dims, mol_count, clu_count, x_ref, c_ref, out_ref, sim_ref, e_ref, t_ref, cc_ref, xc_ref, xu_ref,
           acc_ref, csb_ref, half_buf, a_buf, cs_buf, y_buf, core_buf, send_buf, xr_buf, zs_buf, zr_buf,
           half_sem, a_sem, cs_sem, y_sem, core_sem, xr_sem, zr_sem, gz_sem, gx_sem, gc_sem):
    nx, nz, ny = dims
    mols, clus = x_ref.shape[0], c_ref.shape[0]
    half = clus // 2
    lanes = half // 128
    rows, y = lax.axis_index("rows"), lax.axis_index("cols")
    core = lax.rem(rows, 2)
    z = lax.rem(lax.div(rows, 2), nz)
    x = lax.div(rows, 2 * nz)
    chip = x * nz + z
    other = 1 - core

    def dev(x_at, z_at, core_at):
        return ((x_at * nz + z_at) * 2 + core_at, y)

    def dev_y(k):
        return (rows, k)

    twin = dev(x, z, other)
    away = [(dx, dz) for dx in range(nx) for dz in range(nz) if dx or dz]
    away.sort(key=lambda p: -(min(p[0], nx - p[0]) + min(p[1], nz - p[1])))

    def chip_at(p):
        return lax.rem(x + p[0], nx), lax.rem(z + p[1], nz)

    def near(n):
        return sorted(range(1, n), key=lambda d: -min(d, n - d))

    barrier = pltpu.get_barrier_semaphore()
    pl.semaphore_signal(barrier, inc=1, device_id=twin, device_id_type=MESH)
    for p in away:
        pl.semaphore_signal(barrier, inc=1, device_id=dev(*chip_at(p), core), device_id_type=MESH)
    for d in range(1, ny):
        pl.semaphore_signal(barrier, inc=1, device_id=dev_y(lax.rem(y + d, ny)), device_id_type=MESH)

    def remote(src, dst, send, recv, to):
        return pltpu.make_async_remote_copy(
            src_ref=src, dst_ref=dst, send_sem=send, recv_sem=recv, device_id=to, device_id_type=MESH)

    sent = []

    def start(src, dst, sem, to, keep=True):
        copy = remote(src, dst, sem.at[0], sem.at[1], to)
        copy.start()
        if keep:
            sent.append((src, sem))

    def wait(ref, sem):
        remote(ref, ref, sem.at[0], sem.at[1], twin).wait_recv()

    def at(start_row, size):
        return pl.ds(pl.multiple_of(start_row, size), size)

    step_p = min(256, mols)

    def prep(i, _):
        r = at(i * step_p, step_p)
        hi, lo = split(unit_rows(c_ref[r, :]) * INV_TEMP)
        cc_ref[r, :] = jnp.concatenate([hi, lo, hi, lo], axis=1)
        u = unit_rows(x_ref[r, :])
        xu_ref[r, :] = u
        hi, lo = split(u)
        xc_ref[r, :] = jnp.concatenate([hi, hi, lo, lo], axis=1)
        return 0

    lax.fori_loop(0, mols // step_p, prep, 0)

    row_b, col_b = min(512, clus), min(512, mols)

    def score(i, _):
        r = at(i * row_b, row_b)
        total = None
        for j in range(mols // col_b):
            m = pl.ds(j * col_b, col_b)
            t = lax.dot_general(cc_ref[r, :], xc_ref[m, :], (((1,), (1,)), ((), ())), preferred_element_type=F32)
            e = jnp.exp(t)
            t_ref[r, m] = t
            e_ref[r, m] = e
            part = e[:, 0:128]
            for k in range(1, col_b // 128):
                part = part + e[:, 128 * k:128 * (k + 1)]
            total = part if total is None else total + part
        acc_ref[r, :] = total
        return 0

    lax.fori_loop(0, clus // row_b, score, 0)

    step_r = min(64, half)
    steps = half // step_r
    zero = jnp.zeros((8, mols), F32)

    def col_pass(of, scale):
        def body(i, scale):
            for g in range(step_r // 8):
                r = at(of * half + i * step_r + g * 8, 8)
                p = e_ref[r, :] * scale
                s = p[:, 0:128]
                for k in range(1, mols // 128):
                    s = s + p[:, 128 * k:128 * (k + 1)]
                acc_ref[r, :] = s
            return scale

        lax.fori_loop(0, steps, body, scale)

    def col_vec(of, dst):
        for j in range(lanes):
            dst[j:j + 1, :] = jnp.sum(acc_ref[at(of * half + 128 * j, 128), :].T, axis=0, keepdims=True)

    def spread(of, src):
        for j in range(lanes):
            csb_ref[at(of * half + 128 * j, 128), :] = to_sublanes(src[j:j + 1, :])

    def scaled(r):
        return e_ref[r, :] * jnp.concatenate([csb_ref[r, :]] * (mols // 128), axis=1)

    def row_pass(of, acc):
        def body(i, acc):
            for g in range(step_r // 8):
                acc = acc + scaled(at(of * half + i * step_r + g * 8, 8))
            return acc

        return lax.fori_loop(0, steps, body, acc)

    def sum_cols(slot, value):
        y_buf[slot, y] = value
        for d in near(ny):
            k = lax.rem(y + d, ny)
            start(y_buf.at[slot, y], y_buf.at[slot, y], y_sem.at[slot], dev_y(k))

        def result():
            wait(y_buf.at[slot, pl.ds(0, ny - 1)], y_sem.at[slot])
            total = y_buf[slot, 0]
            for k in range(1, ny):
                total = total + y_buf[slot, k]
            return total

        return result

    for it in range(ITERS):
        if it > 0:
            scale = jnp.broadcast_to(1.0 / mol_count / row_sum, (8, mols))
            col_pass(other, scale)
        else:
            pl.semaphore_wait(barrier, nx * nz + ny - 1)
        col_vec(other, half_buf.at[it, 0])
        start(half_buf.at[it, 0], half_buf.at[it, 1], half_sem.at[it], twin)
        if it > 0:
            col_pass(core, scale)
        mine = a_buf.at[it, chip]
        col_vec(core, mine)
        wait(half_buf.at[it, 1], half_sem.at[it])
        mine[...] = mine[...] + half_buf[it, 1]
        for p in away:
            start(mine, mine, a_sem.at[it], dev(*chip_at(p), core))
        wait(a_buf.at[it, pl.ds(0, nx * nz - 1)], a_sem.at[it])
        col_mass = jnp.sum(a_buf[it], axis=0)
        cs_buf[it, core] = 1.0 / clu_count / col_mass
        start(cs_buf.at[it, core], cs_buf.at[it, core], cs_sem.at[it], twin)
        spread(core, cs_buf.at[it, core])
        acc = row_pass(core, zero)
        wait(cs_buf.at[it, other], cs_sem.at[it])
        spread(other, cs_buf.at[it, other])
        acc = row_pass(other, acc)
        row_sum = sum_cols(it, jnp.sum(acc, axis=0, keepdims=True))()

    inv = 1.0 / row_sum
    for j in range(mols // 128):
        s = slice(128 * j, 128 * (j + 1))
        hi, lo = split(xu_ref[s, :] * to_sublanes(inv[:, s]))
        xc_ref[s, 0:256] = jnp.concatenate([hi, lo], axis=1)

    size = clus // CHUNKS
    part = size // 2
    blk = part // nx
    sub = blk // nz

    def row_at(k, core_at, x_at=0, z_at=0):
        return k * size + core_at * part + x_at * blk + z_at * sub

    def sums(r):
        hi, lo = split(e_ref[r, :])
        p = jnp.dot(jnp.concatenate([hi, lo], axis=0), xc_ref[:, 0:256], preferred_element_type=F32)
        p = p[:, 0:128] + p[:, 128:256]
        return (p[0:part] + p[part:2 * part]) * csb_ref[r, :]

    def to_twin(k):
        return remote(send_buf.at[k, 1], core_buf.at[k], core_sem.at[k, 0], core_sem.at[k, 1], twin)

    def products(k, _):
        send_buf[k, 1] = sums(at(row_at(k, other), part))
        to_twin(k).start()
        send_buf[k, 0] = sums(at(row_at(k, core), part))
        to_twin(k).wait_recv()
        send_buf[k, 0] = send_buf[k, 0] + core_buf[k]
        for d in near(nx):
            to = lax.rem(x + d, nx)
            remote(send_buf.at[k, 0, at(to * blk, blk)], xr_buf.at[k, x], xr_sem.at[k, 0], xr_sem.at[k, 1],
                   dev(to, z, core)).start()
        xr_buf[k, x] = send_buf[k, 0, at(x * blk, blk), :]
        return 0

    lax.fori_loop(0, CHUNKS, products, 0)

    def after_x(k):
        wait(xr_buf.at[k, pl.ds(0, nx - 1)], xr_sem.at[k])
        total = xr_buf[k, 0]
        for j in range(1, nx):
            total = total + xr_buf[k, j]
        zs_buf[k] = total
        for d in near(nz):
            to = lax.rem(z + d, nz)
            start(zs_buf.at[k, at(to * sub, sub)], zr_buf.at[k, z], zr_sem.at[k], dev(x, to, core))
        zr_buf[k, z] = zs_buf[k, at(z * sub, sub), :]

    def after_z(k):
        wait(zr_buf.at[k, pl.ds(0, nz - 1)], zr_sem.at[k])
        total = zr_buf[k, 0]
        for j in range(1, nz):
            total = total + zr_buf[k, j]
        r = at(row_at(k, core, x, z), sub)
        out_ref[r, :] = unit_rows(total)
        for d in near(nz):
            to = lax.rem(z + d, nz)
            start(out_ref.at[r], out_ref.at[r], gz_sem.at[k], dev(x, to, core))

    def forward(k, x_at):
        ref = out_ref.at[at(row_at(k, core, x_at), blk)]
        start(ref, ref, gc_sem.at[k], twin)

    def after_gather_z(k):
        wait(zr_buf.at[k, pl.ds(0, nz - 1)], gz_sem.at[k])
        ref = out_ref.at[at(row_at(k, core, x), blk)]
        for d in near(nx):
            to = lax.rem(x + d, nx)
            start(ref, ref, gx_sem.at[k], dev(to, z, core))
        forward(k, x)

    def after_gather_x(k):
        wait(xr_buf.at[k, pl.ds(0, nx - 1)], gx_sem.at[k])
        for d in range(1, nx):
            forward(k, lax.rem(x + d, nx))

    for k in range(CHUNKS):
        after_x(k)

    def numer_pass(i, acc):
        for g in range(step_r // 8):
            r = at(i * step_r + g * 8, 8)
            acc = acc + scaled(r) * t_ref[r, :]
        return acc

    numer = jnp.sum(lax.fori_loop(0, 2 * steps, numer_pass, zero), axis=0, keepdims=True)
    numer = sum_cols(ITERS, numer)
    for k in range(CHUNKS):
        after_z(k)
    sim_ref[...] = numer() / row_sum * (1.0 / INV_TEMP)
    for k in range(CHUNKS):
        after_gather_z(k)
    for k in range(CHUNKS):
        after_gather_x(k)
    for k in range(CHUNKS):
        wait(core_buf.at[k], gc_sem.at[k])

    for src, sem in sent:
        remote(src, src, sem.at[0], sem.at[1], twin).wait_send()
    for k in range(CHUNKS):
        to_twin(k).wait_send()
        for d in range(1, nx):
            remote(xr_buf.at[k, 0], xr_buf.at[k, 0], xr_sem.at[k, 0], xr_sem.at[k, 1], twin).wait_send()


def local(dims, embeddings, centres):
    nx, nz, ny = dims
    mols, emb = embeddings.shape
    clus = centres.shape[0]
    half = clus // 2
    size = clus // CHUNKS
    part = size // 2
    blk = part // nx
    sub = blk // nz
    dma = pltpu.SemaphoreType.DMA
    new_centres, expected = pl.pallas_call(
        functools.partial(kernel, dims, mols * lax.axis_size("rows"), clus * lax.axis_size("cols")),
        out_shape=(jax.ShapeDtypeStruct((clus, emb), F32), jax.ShapeDtypeStruct((1, mols), F32)),
        in_specs=[pl.BlockSpec(memory_space=pltpu.VMEM)] * 2,
        out_specs=(pl.BlockSpec(memory_space=pltpu.VMEM),) * 2,
        scratch_shapes=[
            pltpu.VMEM((clus, mols), F32),
            pltpu.VMEM((clus, mols), F32),
            pltpu.VMEM((clus, 4 * emb), BF16),
            pltpu.VMEM((mols, 4 * emb), BF16),
            pltpu.VMEM((mols, emb), F32),
            pltpu.VMEM((clus, 128), F32),
            pltpu.VMEM((clus, 128), F32),
            pltpu.VMEM((ITERS, 2, half // 128, 128), F32),
            pltpu.VMEM((ITERS, nx * nz, half // 128, 128), F32),
            pltpu.VMEM((ITERS, 2, half // 128, 128), F32),
            pltpu.VMEM((ITERS + 1, ny, 1, mols), F32),
            pltpu.VMEM((CHUNKS, part, emb), F32),
            pltpu.VMEM((CHUNKS, 2, part, emb), F32),
            pltpu.VMEM((CHUNKS, nx, blk, emb), F32),
            pltpu.VMEM((CHUNKS, blk, emb), F32),
            pltpu.VMEM((CHUNKS, nz, sub, emb), F32),
            dma((ITERS, 2)),
            dma((ITERS, 2)),
            dma((ITERS, 2)),
            dma((ITERS + 1, 2)),
            dma((CHUNKS, 2)),
            dma((CHUNKS, 2)),
            dma((CHUNKS, 2)),
            dma((CHUNKS, 2)),
            dma((CHUNKS, 2)),
            dma((CHUNKS, 2)),
        ],
        compiler_params=pltpu.CompilerParams(
            collective_id=0, has_side_effects=True, vmem_limit_bytes=60 * 1024 * 1024),
        cost_estimate=pl.CostEstimate(flops=2 * 8 * mols * clus * emb, bytes_accessed=4 * 1024 * 1024,
                                      transcendentals=mols * clus),
    )(embeddings, centres)
    return new_centres, expected.reshape(mols)


def solution(mesh, dims=(CHIPS_X, CHIPS_Z, CHIPS_Y)):
    return jax.shard_map(
        functools.partial(local, dims), mesh=mesh, in_specs=(P("rows", None), P("cols", None)),
        out_specs=(P("cols", None), P("rows")), check_vma=False)
```

```python
import functools

import jax
import jax.numpy as jnp
from jax import lax
from jax.experimental import pallas as pl
from jax.experimental.pallas import tpu as pltpu
from jax.sharding import PartitionSpec as P

ITERS = 3
INV_TEMP = 20.0
EPS = 1e-06
F32 = jnp.float32
BF16 = jnp.bfloat16
MESH = pl.DeviceIdType.MESH
CHIPS_X, CHIPS_Z, CHIPS_Y = 4, 8, 4
CHUNKS = 4
Z_FIRST = (0,)


def split(value):
    hi = value.astype(BF16)
    lo = (value - hi.astype(F32)).astype(BF16)
    return hi, lo


def unit_rows(value):
    return value * lax.rsqrt(jnp.sum(value * value, axis=-1, keepdims=True) + EPS)


def to_sublanes(row, width=128):
    return jnp.broadcast_to(row, (width, 128)).T


def kernel(dims, mol_count, clu_count, x_hbm, c_hbm, out_hbm, sim_ref, out_ref, e_ref, t_ref, cc_ref, xc_ref, xu_ref,
           acc_ref, csb_ref, half_buf, a_buf, cs_buf, y_buf, core_buf, send_buf, xr_buf, zs_buf, zr_buf,
           in_sem, out_sem, half_sem, a_sem, cs_sem, y_sem, core_sem, xr_sem, zr_sem, gz_sem, gx_sem, gc_sem):
    nx, nz, ny = dims
    mols, clus = x_hbm.shape[0], c_hbm.shape[0]
    step_p = min(256, mols)
    loads = []
    for i in range(mols // step_p):
        r = pl.ds(i * step_p, step_p)
        for k, (src, dst) in enumerate(((c_hbm, acc_ref), (x_hbm, xu_ref))):
            loads.append(pltpu.make_async_copy(src.at[r], dst.at[r], in_sem.at[i, k]))
            loads[-1].start()
    half = clus // 2
    lanes = half // 128
    rows, y = lax.axis_index("rows"), lax.axis_index("cols")
    core = lax.rem(rows, 2)
    z = lax.rem(lax.div(rows, 2), nz)
    x = lax.div(rows, 2 * nz)
    chip = x * nz + z
    other = 1 - core

    def dev(x_at, z_at, core_at):
        return ((x_at * nz + z_at) * 2 + core_at, y)

    def dev_y(k):
        return (rows, k)

    twin = dev(x, z, other)
    away = [(dx, dz) for dx in range(nx) for dz in range(nz) if dx or dz]
    away.sort(key=lambda p: -(min(p[0], nx - p[0]) + min(p[1], nz - p[1])))

    def chip_at(p):
        return lax.rem(x + p[0], nx), lax.rem(z + p[1], nz)

    def near(n):
        return sorted(range(1, n), key=lambda d: -min(d, n - d))

    barrier = pltpu.get_barrier_semaphore()
    pl.semaphore_signal(barrier, inc=1, device_id=twin, device_id_type=MESH)
    for p in away:
        pl.semaphore_signal(barrier, inc=1, device_id=dev(*chip_at(p), core), device_id_type=MESH)
    for d in range(1, ny):
        pl.semaphore_signal(barrier, inc=1, device_id=dev_y(lax.rem(y + d, ny)), device_id_type=MESH)

    def remote(src, dst, send, recv, to):
        return pltpu.make_async_remote_copy(
            src_ref=src, dst_ref=dst, send_sem=send, recv_sem=recv, device_id=to, device_id_type=MESH)

    sent = []

    def start(src, dst, sem, to, keep=True):
        copy = remote(src, dst, sem.at[0], sem.at[1], to)
        copy.start()
        if keep:
            sent.append((src, sem))

    def wait(ref, sem):
        remote(ref, ref, sem.at[0], sem.at[1], twin).wait_recv()

    def at(start_row, size):
        return pl.ds(pl.multiple_of(start_row, size), size)

    for i in range(mols // step_p):
        r = pl.ds(i * step_p, step_p)
        loads[2 * i].wait()
        cc_ref[r, :] = jnp.concatenate(split(unit_rows(acc_ref[r, :]) * INV_TEMP), axis=1)
        loads[2 * i + 1].wait()
        u = unit_rows(xu_ref[r, :])
        xu_ref[r, :] = u
        xc_ref[r, :] = jnp.concatenate(split(u), axis=1)

    row_b, col_b = min(1024, clus), min(256, mols)

    def score(i, _):
        r = at(i * row_b, row_b)
        total = None
        for j in range(mols // col_b):
            m = pl.ds(j * col_b, col_b)
            c, u = cc_ref[r, :], xc_ref[m, :]
            hi, lo = u[:, 0:128], u[:, 128:256]
            t = lax.dot_general(jnp.concatenate([c, c], axis=1), jnp.concatenate([hi, hi, lo, lo], axis=1),
                                (((1,), (1,)), ((), ())), preferred_element_type=F32)
            e = jnp.exp(t)
            t_ref[r, m] = t
            e_ref[r, m] = e
            part = e[:, 0:128]
            for k in range(1, col_b // 128):
                part = part + e[:, 128 * k:128 * (k + 1)]
            total = part if total is None else total + part
        acc_ref[r, :] = total
        return 0

    lax.fori_loop(0, clus // row_b, score, 0)

    step_r = min(128, half)
    steps = half // step_r
    zero = jnp.zeros((8, mols), F32)

    def col_pass(of, scale):
        def body(i, scale):
            for g in range(step_r // 8):
                r = at(of * half + i * step_r + g * 8, 8)
                p = e_ref[r, :] * scale
                s = p[:, 0:128]
                for k in range(1, mols // 128):
                    s = s + p[:, 128 * k:128 * (k + 1)]
                acc_ref[r, :] = s
            return scale

        lax.fori_loop(0, steps, body, scale)

    def col_vec(of, dst):
        for j in range(lanes):
            dst[j:j + 1, :] = jnp.sum(acc_ref[at(of * half + 128 * j, 128), :].T, axis=0, keepdims=True)

    def spread(of, src):
        for j in range(lanes):
            csb_ref[at(of * half + 128 * j, 128), :] = to_sublanes(src[j:j + 1, :])

    def scaled(r):
        return e_ref[r, :] * jnp.concatenate([csb_ref[r, :]] * (mols // 128), axis=1)

    def row_pass(of, acc):
        def body(i, acc):
            for g in range(step_r // 8):
                acc = acc + scaled(at(of * half + i * step_r + g * 8, 8))
            return acc

        return lax.fori_loop(0, steps, body, acc)

    def sum_cols(slot, value):
        y_buf[slot, y] = value
        for d in near(ny):
            k = lax.rem(y + d, ny)
            start(y_buf.at[slot, y], y_buf.at[slot, y], y_sem.at[slot], dev_y(k))

        def result():
            wait(y_buf.at[slot, pl.ds(0, ny - 1)], y_sem.at[slot])
            total = y_buf[slot, 0]
            for k in range(1, ny):
                total = total + y_buf[slot, k]
            return total

        return result

    for it in range(ITERS):
        if it > 0:
            scale = jnp.broadcast_to(1.0 / mol_count / row_sum, (8, mols))
            col_pass(other, scale)
        else:
            pl.semaphore_wait(barrier, nx * nz + ny - 1)
        col_vec(other, half_buf.at[it, 0])
        start(half_buf.at[it, 0], half_buf.at[it, 1], half_sem.at[it], twin)
        if it > 0:
            col_pass(core, scale)
        mine = a_buf.at[it, chip]
        col_vec(core, mine)
        wait(half_buf.at[it, 1], half_sem.at[it])
        mine[...] = mine[...] + half_buf[it, 1]
        for p in away:
            start(mine, mine, a_sem.at[it], dev(*chip_at(p), core))
        wait(a_buf.at[it, pl.ds(0, nx * nz - 1)], a_sem.at[it])
        col_mass = jnp.sum(a_buf[it], axis=0)
        cs_buf[it, core] = 1.0 / clu_count / col_mass
        start(cs_buf.at[it, core], cs_buf.at[it, core], cs_sem.at[it], twin)
        spread(core, cs_buf.at[it, core])
        acc = row_pass(core, zero)
        wait(cs_buf.at[it, other], cs_sem.at[it])
        spread(other, cs_buf.at[it, other])
        acc = row_pass(other, acc)
        row_sum = sum_cols(it, jnp.sum(acc, axis=0, keepdims=True))()

    inv = 1.0 / row_sum
    for j in range(mols // 128):
        s = slice(128 * j, 128 * (j + 1))
        hi, lo = split(xu_ref[s, :] * to_sublanes(inv[:, s]))
        xc_ref[s, :] = jnp.concatenate([hi, lo], axis=1)

    size = clus // CHUNKS
    part = size // 2

    class Axis:
        def __init__(self, n, place, at_place):
            self.n, self.place, self.at_place = n, place, at_place

        def peers(self):
            for d in near(self.n):
                to = lax.rem(self.place + d, self.n)
                yield to, self.at_place(to)

    x_axis = Axis(nx, x, lambda k: dev(k, z, core))
    z_axis = Axis(nz, z, lambda k: dev(x, k, core))
    sub = part // (nx * nz)

    def axes(k):
        return (z_axis, x_axis) if k in Z_FIRST else (x_axis, z_axis)

    def row_at(k, core_at, first=0, second=0):
        return k * size + core_at * part + first * (part // axes(k)[0].n) + second * sub

    def sums(r):
        n = r.size
        p = jnp.dot(jnp.concatenate(split(e_ref[r, :]), axis=0), xc_ref[...], preferred_element_type=F32)
        p = p[:, 0:128] + p[:, 128:256]
        return (p[0:n] + p[n:2 * n]) * csb_ref[r, :]

    def to_twin(k):
        return remote(send_buf.at[k, other], core_buf.at[k], core_sem.at[k, 0], core_sem.at[k, 1], twin)

    def scatter(k):
        one = axes(k)[0]
        blk = part // one.n
        to_twin(k).wait_recv()
        send_buf[k, core] = send_buf[k, core] + core_buf[k]
        for to, peer in one.peers():
            start(send_buf.at[k, core, at(to * blk, blk)], xr_buf.at[k, at(one.place * blk, blk)], xr_sem.at[k], peer,
                  False)
        xr_buf[k, at(one.place * blk, blk), :] = send_buf[k, core, at(one.place * blk, blk), :]

    last = CHUNKS - 1

    def products(k, _):
        both = sums(at(k * size, size))
        send_buf[k, 0] = both[0:part]
        send_buf[k, 1] = both[part:size]
        to_twin(k).start()
        for done in range(last - 1):
            @pl.when(k == done + 1)
            def _():
                scatter(done)

        return 0

    lax.fori_loop(0, last, products, 0)
    send_buf[last, other] = sums(at(row_at(last, other), part))
    to_twin(last).start()
    scatter(last - 1)
    send_buf[last, core] = sums(at(row_at(last, core), part))
    scatter(last)

    def total_of(ref, n):
        rows = ref.shape[0] // n
        total = ref[0:rows, :]
        for j in range(1, n):
            total = total + ref[j * rows:(j + 1) * rows, :]
        return total

    def after_first(k):
        one, two = axes(k)
        blk = part // one.n
        wait(xr_buf.at[k, pl.ds(0, part - blk)], xr_sem.at[k])
        zs_buf[k, 0:blk, :] = total_of(xr_buf.at[k], one.n)
        for to, peer in two.peers():
            start(zs_buf.at[k, at(to * sub, sub)], zr_buf.at[k, at(two.place * sub, sub)], zr_sem.at[k], peer)
        zr_buf[k, at(two.place * sub, sub), :] = zs_buf[k, at(two.place * sub, sub), :]

    def after_second(k):
        one, two = axes(k)
        blk = part // one.n
        wait(zr_buf.at[k, pl.ds(0, blk - sub)], zr_sem.at[k])
        r = at(row_at(k, core, one.place, two.place), sub)
        out_ref[r, :] = unit_rows(total_of(zr_buf.at[k, pl.ds(0, blk)], two.n))
        for _, peer in two.peers():
            start(out_ref.at[r], out_ref.at[r], gz_sem.at[k], peer)

    def after_gather_second(k):
        one = axes(k)[0]
        blk = part // one.n
        wait(zr_buf.at[k, pl.ds(0, blk - sub)], gz_sem.at[k])
        ref = out_ref.at[at(row_at(k, core, one.place), blk)]
        for _, peer in one.peers():
            start(ref, ref, gx_sem.at[k], peer)

    def after_gather_first(k):
        wait(xr_buf.at[k, pl.ds(0, part - part // axes(k)[0].n)], gx_sem.at[k])
        ref = out_ref.at[at(row_at(k, core), part)]
        start(ref, ref, gc_sem.at[k], twin)

    def leave(k):
        r = at(k * size, size)
        return pltpu.make_async_copy(out_ref.at[r], out_hbm.at[r], out_sem.at[k])

    order = [k for k in range(CHUNKS) if k not in Z_FIRST] + list(Z_FIRST)
    for k in order:
        after_first(k)

    def numer_pass(i, acc):
        for g in range(step_r // 8):
            r = at(i * step_r + g * 8, 8)
            acc = acc + scaled(r) * t_ref[r, :]
        return acc

    numer = jnp.sum(lax.fori_loop(0, 2 * steps, numer_pass, zero), axis=0, keepdims=True)
    numer = sum_cols(ITERS, numer)
    order = list(Z_FIRST) + [k for k in range(CHUNKS) if k not in Z_FIRST]
    for k in order:
        after_second(k)
    sim_ref[...] = numer() / row_sum * (1.0 / INV_TEMP)
    for k in order:
        after_gather_second(k)
    order = [k for k in range(CHUNKS - 1) if k not in Z_FIRST] + list(Z_FIRST) + [CHUNKS - 1]
    done = None
    for k in order + [None]:
        if k is not None:
            after_gather_first(k)
        if done is not None:
            wait(core_buf.at[done], gc_sem.at[done])
            leave(done).start()
        done = k

    for src, sem in sent:
        remote(src, src, sem.at[0], sem.at[1], twin).wait_send()
    for k in range(CHUNKS):
        to_twin(k).wait_send()
        ref = xr_buf.at[k, pl.ds(0, part - part // axes(k)[0].n)]
        remote(ref, ref, xr_sem.at[k, 0], xr_sem.at[k, 1], twin).wait_send()
        leave(k).wait()


def hand_out(centres_ref, sim_ref, out_ref, expected_ref, sem):
    rows = out_ref.shape[0] // 4
    copies = [pltpu.make_async_copy(sim_ref, expected_ref, sem.at[4])]
    for i in range(4):
        r = pl.ds(i * rows, rows)
        copies.append(pltpu.make_async_copy(centres_ref.at[r], out_ref.at[r], sem.at[i]))
    for copy in copies:
        copy.start()
    for copy in copies:
        copy.wait()


def local(dims, embeddings, centres):
    nx, nz, ny = dims
    mols, emb = embeddings.shape
    clus = centres.shape[0]
    half = clus // 2
    size = clus // CHUNKS
    part = size // 2
    dma = pltpu.SemaphoreType.DMA
    new_centres, expected = pl.pallas_call(
        functools.partial(kernel, dims, mols * lax.axis_size("rows"), clus * lax.axis_size("cols")),
        out_shape=(jax.ShapeDtypeStruct((clus, emb), F32), jax.ShapeDtypeStruct((1, mols), F32)),
        in_specs=[pl.BlockSpec(memory_space=pl.ANY)] * 2,
        out_specs=(pl.BlockSpec(memory_space=pl.ANY), pl.BlockSpec(memory_space=pltpu.VMEM)),
        scratch_shapes=[
            pltpu.VMEM((clus, emb), F32),
            pltpu.VMEM((clus, mols), F32),
            pltpu.VMEM((clus, mols), F32),
            pltpu.VMEM((clus, 2 * emb), BF16),
            pltpu.VMEM((mols, 2 * emb), BF16),
            pltpu.VMEM((mols, emb), F32),
            pltpu.VMEM((clus, 128), F32),
            pltpu.VMEM((clus, 128), F32),
            pltpu.VMEM((ITERS, 2, half // 128, 128), F32),
            pltpu.VMEM((ITERS, nx * nz, half // 128, 128), F32),
            pltpu.VMEM((ITERS, 2, half // 128, 128), F32),
            pltpu.VMEM((ITERS + 1, ny, 1, mols), F32),
            pltpu.VMEM((CHUNKS, part, emb), F32),
            pltpu.VMEM((CHUNKS, 2, part, emb), F32),
            pltpu.VMEM((CHUNKS, part, emb), F32),
            pltpu.VMEM((CHUNKS, part // min(nx, nz), emb), F32),
            pltpu.VMEM((CHUNKS, part // min(nx, nz), emb), F32),
            dma((mols // min(256, mols), 2)),
            dma((CHUNKS,)),
            dma((ITERS, 2)),
            dma((ITERS, 2)),
            dma((ITERS, 2)),
            dma((ITERS + 1, 2)),
            dma((CHUNKS, 2)),
            dma((CHUNKS, 2)),
            dma((CHUNKS, 2)),
            dma((CHUNKS, 2)),
            dma((CHUNKS, 2)),
            dma((CHUNKS, 2)),
        ],
        compiler_params=pltpu.CompilerParams(
            collective_id=0, has_side_effects=True, vmem_limit_bytes=62 * 1024 * 1024),
        cost_estimate=pl.CostEstimate(flops=2 * 8 * mols * clus * emb, bytes_accessed=4 * 1024 * 1024,
                                      transcendentals=mols * clus),
    )(embeddings, centres)
    new_centres, expected = pl.pallas_call(
        hand_out,
        out_shape=(jax.ShapeDtypeStruct((clus, emb), F32), jax.ShapeDtypeStruct((1, mols), F32)),
        in_specs=[pl.BlockSpec(memory_space=pltpu.VMEM)] * 2,
        out_specs=(pl.BlockSpec(memory_space=pl.ANY),) * 2,
        scratch_shapes=[dma((5,))],
    )(new_centres, expected)
    return new_centres, expected.reshape(mols)


def solution(mesh, dims=(CHIPS_X, CHIPS_Z, CHIPS_Y)):
    return jax.shard_map(
        functools.partial(local, dims), mesh=mesh, in_specs=(P("rows", None), P("cols", None)),
        out_specs=(P("cols", None), P("rows")), check_vma=False)
```

```python
import functools

import jax
import jax.numpy as jnp
from jax import lax
from jax.experimental import pallas as pl
from jax.experimental.pallas import tpu as pltpu
from jax.sharding import PartitionSpec as P

ITERS = 3
INV_TEMP = 20.0
EPS = 1e-06
F32 = jnp.float32
BF16 = jnp.bfloat16
MESH = pl.DeviceIdType.MESH
CHIPS_X, CHIPS_Z, CHIPS_Y = 4, 8, 4
CHUNKS = 4
Z_FIRST = ()
ONE_SHOT = (2, 3)


def split(value):
    hi = value.astype(BF16)
    lo = (value - hi.astype(F32)).astype(BF16)
    return hi, lo


def unit_rows(value):
    return value * lax.rsqrt(jnp.sum(value * value, axis=-1, keepdims=True) + EPS)


def to_sublanes(row, width=128):
    return jnp.broadcast_to(row, (width, 128)).T


def kernel(dims, mol_count, clu_count, x_hbm, c_hbm, out_hbm, sim_ref, out_ref, e_ref, t_ref, cc_ref, xc_ref, xu_ref,
           acc_ref, csb_ref, half_buf, a_buf, cs_buf, y_buf, core_buf, send_buf, xr_buf, zs_buf, zr_buf,
           in_sem, out_sem, half_sem, a_sem, cs_sem, y_sem, core_sem, xr_sem, zr_sem, gz_sem, gx_sem, gc_sem):
    nx, nz, ny = dims
    mols, clus = x_hbm.shape[0], c_hbm.shape[0]
    step_p = min(256, mols)
    loads = []
    for i in range(mols // step_p):
        r = pl.ds(i * step_p, step_p)
        for k, (src, dst) in enumerate(((c_hbm, acc_ref), (x_hbm, xu_ref))):
            loads.append(pltpu.make_async_copy(src.at[r], dst.at[r], in_sem.at[i, k]))
            loads[-1].start()
    half = clus // 2
    lanes = half // 128
    rows, y = lax.axis_index("rows"), lax.axis_index("cols")
    core = lax.rem(rows, 2)
    z = lax.rem(lax.div(rows, 2), nz)
    x = lax.div(rows, 2 * nz)
    chip = x * nz + z
    other = 1 - core

    def dev(x_at, z_at, core_at):
        return ((x_at * nz + z_at) * 2 + core_at, y)

    def dev_y(k):
        return (rows, k)

    twin = dev(x, z, other)
    away = [(dx, dz) for dx in range(nx) for dz in range(nz) if dx or dz]
    away.sort(key=lambda p: -(min(p[0], nx - p[0]) + min(p[1], nz - p[1])))

    def chip_at(p):
        return lax.rem(x + p[0], nx), lax.rem(z + p[1], nz)

    def near(n):
        return sorted(range(1, n), key=lambda d: -min(d, n - d))

    barrier = pltpu.get_barrier_semaphore()
    pl.semaphore_signal(barrier, inc=1, device_id=twin, device_id_type=MESH)
    for p in away:
        pl.semaphore_signal(barrier, inc=1, device_id=dev(*chip_at(p), core), device_id_type=MESH)
    for d in range(1, ny):
        pl.semaphore_signal(barrier, inc=1, device_id=dev_y(lax.rem(y + d, ny)), device_id_type=MESH)

    def remote(src, dst, send, recv, to):
        return pltpu.make_async_remote_copy(
            src_ref=src, dst_ref=dst, send_sem=send, recv_sem=recv, device_id=to, device_id_type=MESH)

    def start(src, dst, sem, to):
        remote(src, dst, sem.at[0], sem.at[1], to).start()

    received = []

    def wait(ref, sem):
        remote(ref, ref, sem.at[0], sem.at[1], twin).wait_recv()
        received.append((ref, sem))

    def drain():
        for ref, sem in received:
            remote(ref, ref, sem.at[0], sem.at[1], twin).wait_send()
        received.clear()

    def at(start_row, size):
        return pl.ds(pl.multiple_of(start_row, size), size)

    for i in range(mols // step_p):
        r = pl.ds(i * step_p, step_p)
        loads[2 * i].wait()
        cc_ref[r, :] = jnp.concatenate(split(unit_rows(acc_ref[r, :]) * INV_TEMP), axis=1)
        loads[2 * i + 1].wait()
        u = unit_rows(xu_ref[r, :])
        xu_ref[r, :] = u
        xc_ref[r, :] = jnp.concatenate(split(u), axis=1)

    row_b, col_b = min(1024, clus), min(256, mols)

    def score(i, _):
        r = at(i * row_b, row_b)
        total = None
        for j in range(mols // col_b):
            m = pl.ds(j * col_b, col_b)
            c, u = cc_ref[r, :], xc_ref[m, :]
            hi, lo = u[:, 0:128], u[:, 128:256]
            t = lax.dot_general(jnp.concatenate([c, c], axis=1), jnp.concatenate([hi, hi, lo, lo], axis=1),
                                (((1,), (1,)), ((), ())), preferred_element_type=F32)
            e = jnp.exp(t)
            t_ref[r, m] = t
            e_ref[r, m] = e
            part = e[:, 0:128]
            for k in range(1, col_b // 128):
                part = part + e[:, 128 * k:128 * (k + 1)]
            total = part if total is None else total + part
        acc_ref[r, :] = total
        return 0

    lax.fori_loop(0, clus // row_b, score, 0)

    step_r = min(256, half)
    steps = half // step_r
    zero = jnp.zeros((8, mols), F32)

    def col_pass(of, scale):
        def body(i, scale):
            for g in range(step_r // 8):
                r = at(of * half + i * step_r + g * 8, 8)
                p = e_ref[r, :] * scale
                s = p[:, 0:128]
                for k in range(1, mols // 128):
                    s = s + p[:, 128 * k:128 * (k + 1)]
                acc_ref[r, :] = s
            return scale

        lax.fori_loop(0, steps, body, scale)

    def col_vec(of, dst):
        for j in range(lanes):
            dst[j:j + 1, :] = jnp.sum(acc_ref[at(of * half + 128 * j, 128), :].T, axis=0, keepdims=True)

    def spread(of, src):
        for j in range(lanes):
            csb_ref[at(of * half + 128 * j, 128), :] = to_sublanes(src[j:j + 1, :])

    def scaled(r):
        return e_ref[r, :] * jnp.concatenate([csb_ref[r, :]] * (mols // 128), axis=1)

    def row_pass(of, acc):
        def body(i, acc):
            for g in range(step_r // 8):
                acc = acc + scaled(at(of * half + i * step_r + g * 8, 8))
            return acc

        return lax.fori_loop(0, steps, body, acc)

    def sum_cols(slot, value):
        y_buf[slot, y] = value
        for d in near(ny):
            k = lax.rem(y + d, ny)
            start(y_buf.at[slot, y], y_buf.at[slot, y], y_sem.at[slot], dev_y(k))

        def result():
            wait(y_buf.at[slot, pl.ds(0, ny - 1)], y_sem.at[slot])
            total = y_buf[slot, 0]
            for k in range(1, ny):
                total = total + y_buf[slot, k]
            return total

        return result

    for it in range(ITERS):
        if it > 0:
            scale = jnp.broadcast_to(1.0 / mol_count / row_sum, (8, mols))
            col_pass(other, scale)
        else:
            pl.semaphore_wait(barrier, nx * nz + ny - 1)
        col_vec(other, half_buf.at[it, 0])
        start(half_buf.at[it, 0], half_buf.at[it, 1], half_sem.at[it], twin)
        if it > 0:
            col_pass(core, scale)
        mine = a_buf.at[it, chip]
        col_vec(core, mine)
        wait(half_buf.at[it, 1], half_sem.at[it])
        mine[...] = mine[...] + half_buf[it, 1]
        for p in away:
            start(mine, mine, a_sem.at[it], dev(*chip_at(p), core))
        wait(a_buf.at[it, pl.ds(0, nx * nz - 1)], a_sem.at[it])
        col_mass = jnp.sum(a_buf[it], axis=0)
        cs_buf[it, core] = 1.0 / clu_count / col_mass
        start(cs_buf.at[it, core], cs_buf.at[it, core], cs_sem.at[it], twin)
        spread(core, cs_buf.at[it, core])
        acc = row_pass(core, zero)
        wait(cs_buf.at[it, other], cs_sem.at[it])
        spread(other, cs_buf.at[it, other])
        acc = row_pass(other, acc)
        row_sum = sum_cols(it, jnp.sum(acc, axis=0, keepdims=True))()

    inv = 1.0 / row_sum
    for j in range(mols // 128):
        s = slice(128 * j, 128 * (j + 1))
        hi, lo = split(xu_ref[s, :] * to_sublanes(inv[:, s]))
        xc_ref[s, :] = jnp.concatenate([hi, lo], axis=1)

    size = clus // CHUNKS
    part = size // 2

    class Axis:
        def __init__(self, n, place, at_place):
            self.n, self.place, self.at_place = n, place, at_place

        def peers(self):
            for d in near(self.n):
                to = lax.rem(self.place + d, self.n)
                yield to, self.at_place(to)

    x_axis = Axis(nx, x, lambda k: dev(k, z, core))
    z_axis = Axis(nz, z, lambda k: dev(x, k, core))
    sub = part // (nx * nz)

    def axes(k):
        return (z_axis, x_axis) if k in Z_FIRST else (x_axis, z_axis)

    def row_at(k, core_at, first=0, second=0):
        return k * size + core_at * part + first * (part // axes(k)[0].n) + second * sub

    def sums(r):
        n = r.size
        p = jnp.dot(jnp.concatenate(split(e_ref[r, :]), axis=0), xc_ref[...], preferred_element_type=F32)
        p = p[:, 0:128] + p[:, 128:256]
        return (p[0:n] + p[n:2 * n]) * csb_ref[r, :]

    def to_twin(k):
        return remote(send_buf.at[k, other], core_buf.at[k], core_sem.at[k, 0], core_sem.at[k, 1], twin)

    def scatter(k):
        one = axes(k)[0]
        blk = part // one.n
        to_twin(k).wait_recv()
        send_buf[k, core] = send_buf[k, core] + core_buf[k]
        for to, peer in one.peers():
            start(send_buf.at[k, core, at(to * blk, blk)], xr_buf.at[k, at(one.place * blk, blk)], xr_sem.at[k], peer)
        xr_buf[k, at(one.place * blk, blk), :] = send_buf[k, core, at(one.place * blk, blk), :]

    last = CHUNKS - 1

    def products(k, _):
        both = sums(at(k * size, size))
        send_buf[k, 0] = both[0:part]
        send_buf[k, 1] = both[part:size]
        to_twin(k).start()
        for done in range(last - 1):
            @pl.when(k == done + 1)
            def _():
                scatter(done)

        return 0

    lax.fori_loop(0, last, products, 0)
    send_buf[last, other] = sums(at(row_at(last, other), part))
    to_twin(last).start()
    scatter(last - 1)
    send_buf[last, core] = sums(at(row_at(last, core), part))
    scatter(last)

    def total_of(ref, n):
        rows = ref.shape[0] // n
        total = ref[0:rows, :]
        for j in range(1, n):
            total = total + ref[j * rows:(j + 1) * rows, :]
        return total

    def after_first(k):
        one, two = axes(k)
        blk = part // one.n
        wait(xr_buf.at[k, pl.ds(0, part - blk)], xr_sem.at[k])
        zs_buf[k, 0:blk, :] = total_of(xr_buf.at[k], one.n)
        for to, peer in two.peers():
            start(zs_buf.at[k, at(to * sub, sub)], zr_buf.at[k, at(two.place * sub, sub)], zr_sem.at[k], peer)
        zr_buf[k, at(two.place * sub, sub), :] = zs_buf[k, at(two.place * sub, sub), :]

    def after_second(k):
        one, two = axes(k)
        blk = part // one.n
        wait(zr_buf.at[k, pl.ds(0, blk - sub)], zr_sem.at[k])
        r = at(row_at(k, core, one.place, two.place), sub)
        out_ref[r, :] = unit_rows(total_of(zr_buf.at[k, pl.ds(0, blk)], two.n))
        if k in ONE_SHOT:
            for p in away:
                start(out_ref.at[r], out_ref.at[r], gx_sem.at[k], dev(*chip_at(p), core))
            return
        for _, peer in two.peers():
            start(out_ref.at[r], out_ref.at[r], gz_sem.at[k], peer)

    def after_gather_second(k):
        one = axes(k)[0]
        blk = part // one.n
        wait(zr_buf.at[k, pl.ds(0, blk - sub)], gz_sem.at[k])
        ref = out_ref.at[at(row_at(k, core, one.place), blk)]
        for _, peer in one.peers():
            start(ref, ref, gx_sem.at[k], peer)

    def after_gather_first(k):
        own = sub if k in ONE_SHOT else part // axes(k)[0].n
        wait(xr_buf.at[k, pl.ds(0, part - own)], gx_sem.at[k])
        ref = out_ref.at[at(row_at(k, core), part)]
        start(ref, ref, gc_sem.at[k], twin)

    def leave(k):
        r = at(k * size, size)
        return pltpu.make_async_copy(out_ref.at[r], out_hbm.at[r], out_sem.at[k])

    def numer_pass(i, acc):
        for g in range(step_r // 8):
            r = at(i * step_r + g * 8, 8)
            acc = acc + scaled(r) * t_ref[r, :]
        return acc

    pieces = 4
    numer = zero

    def numer_piece(i):
        return lax.fori_loop(2 * steps * i // pieces, 2 * steps * (i + 1) // pieces, numer_pass, numer)

    def end(k):
        wait(core_buf.at[k], gc_sem.at[k])
        leave(k).start()

    after_first(0)
    numer = numer_piece(0)
    after_first(1)
    numer = numer_piece(1)
    after_first(2)
    numer = numer_piece(2)
    after_first(3)
    after_second(0)
    numer = numer_piece(3)
    numer = sum_cols(ITERS, jnp.sum(numer, axis=0, keepdims=True))
    after_second(1)
    after_second(2)
    after_second(3)
    after_gather_second(0)
    after_gather_second(1)
    sim_ref[...] = numer() / row_sum * (1.0 / INV_TEMP)
    after_gather_first(0)
    after_gather_first(1)
    end(0)
    after_gather_first(2)
    end(1)
    after_gather_first(3)
    end(2)
    end(3)

    drain()
    for k in range(CHUNKS):
        to_twin(k).wait_send()
        leave(k).wait()


def hand_out(centres_ref, sim_ref, out_ref, expected_ref, sem):
    rows = out_ref.shape[0] // 4
    copies = [pltpu.make_async_copy(sim_ref, expected_ref, sem.at[4])]
    for i in range(4):
        r = pl.ds(i * rows, rows)
        copies.append(pltpu.make_async_copy(centres_ref.at[r], out_ref.at[r], sem.at[i]))
    for copy in copies:
        copy.start()
    for copy in copies:
        copy.wait()


def local(dims, embeddings, centres):
    nx, nz, ny = dims
    mols, emb = embeddings.shape
    clus = centres.shape[0]
    half = clus // 2
    size = clus // CHUNKS
    part = size // 2
    dma = pltpu.SemaphoreType.DMA
    new_centres, expected = pl.pallas_call(
        functools.partial(kernel, dims, mols * lax.axis_size("rows"), clus * lax.axis_size("cols")),
        out_shape=(jax.ShapeDtypeStruct((clus, emb), F32), jax.ShapeDtypeStruct((1, mols), F32)),
        in_specs=[pl.BlockSpec(memory_space=pl.ANY)] * 2,
        out_specs=(pl.BlockSpec(memory_space=pl.ANY), pl.BlockSpec(memory_space=pltpu.VMEM)),
        scratch_shapes=[
            pltpu.VMEM((clus, emb), F32),
            pltpu.VMEM((clus, mols), F32),
            pltpu.VMEM((clus, mols), F32),
            pltpu.VMEM((clus, 2 * emb), BF16),
            pltpu.VMEM((mols, 2 * emb), BF16),
            pltpu.VMEM((mols, emb), F32),
            pltpu.VMEM((clus, 128), F32),
            pltpu.VMEM((clus, 128), F32),
            pltpu.VMEM((ITERS, 2, half // 128, 128), F32),
            pltpu.VMEM((ITERS, nx * nz, half // 128, 128), F32),
            pltpu.VMEM((ITERS, 2, half // 128, 128), F32),
            pltpu.VMEM((ITERS + 1, ny, 1, mols), F32),
            pltpu.VMEM((CHUNKS, part, emb), F32),
            pltpu.VMEM((CHUNKS, 2, part, emb), F32),
            pltpu.VMEM((CHUNKS, part, emb), F32),
            pltpu.VMEM((CHUNKS, part // min(nx, nz), emb), F32),
            pltpu.VMEM((CHUNKS, part // min(nx, nz), emb), F32),
            dma((mols // min(256, mols), 2)),
            dma((CHUNKS,)),
            dma((ITERS, 2)),
            dma((ITERS, 2)),
            dma((ITERS, 2)),
            dma((ITERS + 1, 2)),
            dma((CHUNKS, 2)),
            dma((CHUNKS, 2)),
            dma((CHUNKS, 2)),
            dma((CHUNKS, 2)),
            dma((CHUNKS, 2)),
            dma((CHUNKS, 2)),
        ],
        compiler_params=pltpu.CompilerParams(
            collective_id=0, has_side_effects=True, vmem_limit_bytes=62 * 1024 * 1024),
        cost_estimate=pl.CostEstimate(flops=2 * 8 * mols * clus * emb, bytes_accessed=4 * 1024 * 1024,
                                      transcendentals=mols * clus),
    )(embeddings, centres)
    new_centres, expected = pl.pallas_call(
        hand_out,
        out_shape=(jax.ShapeDtypeStruct((clus, emb), F32), jax.ShapeDtypeStruct((1, mols), F32)),
        in_specs=[pl.BlockSpec(memory_space=pltpu.VMEM)] * 2,
        out_specs=(pl.BlockSpec(memory_space=pl.ANY),) * 2,
        scratch_shapes=[dma((5,))],
    )(new_centres, expected)
    return new_centres, expected.reshape(mols)


def solution(mesh, dims=(CHIPS_X, CHIPS_Z, CHIPS_Y)):
    return jax.shard_map(
        functools.partial(local, dims), mesh=mesh, in_specs=(P("rows", None), P("cols", None)),
        out_specs=(P("cols", None), P("rows")), check_vma=False)
```

```python
import functools

import jax
import jax.numpy as jnp
from jax import lax
from jax.experimental import pallas as pl
from jax.experimental.pallas import tpu as pltpu
from jax.sharding import PartitionSpec as P

ITERS = 3
INV_TEMP = 20.0
EPS = 1e-06
F32 = jnp.float32
BF16 = jnp.bfloat16
MESH = pl.DeviceIdType.MESH
CHIPS_X, CHIPS_Z, CHIPS_Y = 4, 8, 4
CHUNKS = 4
Z_FIRST = ()
ONE_SHOT = (2, 3)


def split(value):
    hi = value.astype(BF16)
    lo = (value - hi.astype(F32)).astype(BF16)
    return hi, lo


def unit_rows(value):
    return value * lax.rsqrt(jnp.sum(value * value, axis=-1, keepdims=True) + EPS)


def to_sublanes(row, width=128):
    return jnp.broadcast_to(row, (width, 128)).T


def kernel(dims, mol_count, clu_count, x_hbm, c_hbm, out_hbm, sim_ref, out_ref, e_ref, t_ref, cc_ref, xc_ref, xu_ref,
           acc_ref, csb_ref, half_buf, a_buf, cs_buf, y_buf, core_buf, send_buf, xr_buf, zs_buf, zr_buf,
           in_sem, out_sem, half_sem, a_sem, cs_sem, y_sem, core_sem, xr_sem, zr_sem, gz_sem, gx_sem, gc_sem):
    nx, nz, ny = dims
    mols, clus = x_hbm.shape[0], c_hbm.shape[0]
    step_p = min(256, mols)
    loads = []
    for i in range(mols // step_p):
        r = pl.ds(i * step_p, step_p)
        for k, (src, dst) in enumerate(((c_hbm, acc_ref), (x_hbm, xu_ref))):
            loads.append(pltpu.make_async_copy(src.at[r], dst.at[r], in_sem.at[i, k]))
            loads[-1].start()
    half = clus // 2
    lanes = half // 128
    rows, y = lax.axis_index("rows"), lax.axis_index("cols")
    core = lax.rem(rows, 2)
    z = lax.rem(lax.div(rows, 2), nz)
    x = lax.div(rows, 2 * nz)
    chip = x * nz + z
    other = 1 - core

    def dev(x_at, z_at, core_at):
        return ((x_at * nz + z_at) * 2 + core_at, y)

    def dev_y(k):
        return (rows, k)

    twin = dev(x, z, other)
    away = [(dx, dz) for dx in range(nx) for dz in range(nz) if dx or dz]
    away.sort(key=lambda p: -(min(p[0], nx - p[0]) + min(p[1], nz - p[1])))

    def chip_at(p):
        return lax.rem(x + p[0], nx), lax.rem(z + p[1], nz)

    def near(n):
        return sorted(range(1, n), key=lambda d: -min(d, n - d))

    barrier = pltpu.get_barrier_semaphore()
    pl.semaphore_signal(barrier, inc=1, device_id=twin, device_id_type=MESH)
    for p in away:
        pl.semaphore_signal(barrier, inc=1, device_id=dev(*chip_at(p), core), device_id_type=MESH)
    for d in range(1, ny):
        pl.semaphore_signal(barrier, inc=1, device_id=dev_y(lax.rem(y + d, ny)), device_id_type=MESH)

    def remote(src, dst, send, recv, to):
        return pltpu.make_async_remote_copy(
            src_ref=src, dst_ref=dst, send_sem=send, recv_sem=recv, device_id=to, device_id_type=MESH)

    def start(src, dst, sem, to):
        remote(src, dst, sem.at[0], sem.at[1], to).start()

    received = []

    def wait(ref, sem):
        remote(ref, ref, sem.at[0], sem.at[1], twin).wait_recv()
        received.append((ref, sem))

    def drain():
        for ref, sem in received:
            remote(ref, ref, sem.at[0], sem.at[1], twin).wait_send()
        received.clear()

    def at(start_row, size):
        return pl.ds(pl.multiple_of(start_row, size), size)

    for i in range(mols // step_p):
        r = pl.ds(i * step_p, step_p)
        loads[2 * i].wait()
        cc_ref[r, :] = jnp.concatenate(split(unit_rows(acc_ref[r, :]) * INV_TEMP), axis=1)
        loads[2 * i + 1].wait()
        u = unit_rows(xu_ref[r, :])
        xu_ref[r, :] = u
        xc_ref[r, :] = jnp.concatenate(split(u), axis=1)

    row_b, col_b = min(1024, clus), min(256, mols)

    def score(i, _):
        r = at(i * row_b, row_b)
        total = None
        for j in range(mols // col_b):
            m = pl.ds(j * col_b, col_b)
            c, u = cc_ref[r, :], xc_ref[m, :]
            hi, lo = u[:, 0:128], u[:, 128:256]
            t = lax.dot_general(jnp.concatenate([c, c], axis=1), jnp.concatenate([hi, hi, lo, lo], axis=1),
                                (((1,), (1,)), ((), ())), preferred_element_type=F32)
            e = jnp.exp(t)
            t_ref[r, m] = t
            e_ref[r, m] = e
            part = e[:, 0:128]
            for k in range(1, col_b // 128):
                part = part + e[:, 128 * k:128 * (k + 1)]
            total = part if total is None else total + part
        acc_ref[r, :] = total
        return 0

    lax.fori_loop(0, clus // row_b, score, 0)

    step_r = min(512, half)
    steps = half // step_r
    zero = jnp.zeros((8, mols), F32)

    def col_pass(of, scale):
        def body(i, scale):
            for g in range(step_r // 8):
                r = at(of * half + i * step_r + g * 8, 8)
                p = e_ref[r, :] * scale
                s = p[:, 0:128]
                for k in range(1, mols // 128):
                    s = s + p[:, 128 * k:128 * (k + 1)]
                acc_ref[r, :] = s
            return scale

        lax.fori_loop(0, steps, body, scale)

    def col_vec(of, dst):
        for j in range(lanes):
            dst[j:j + 1, :] = jnp.sum(acc_ref[at(of * half + 128 * j, 128), :].T, axis=0, keepdims=True)

    def spread(of, src):
        for j in range(lanes):
            csb_ref[at(of * half + 128 * j, 128), :] = to_sublanes(src[j:j + 1, :])

    def scaled(r):
        return e_ref[r, :] * jnp.concatenate([csb_ref[r, :]] * (mols // 128), axis=1)

    def row_pass(of, acc):
        def body(i, acc):
            for g in range(step_r // 8):
                acc = acc + scaled(at(of * half + i * step_r + g * 8, 8))
            return acc

        return lax.fori_loop(0, steps, body, acc)

    def sum_cols(slot, value):
        y_buf[slot, y] = value
        for d in near(ny):
            k = lax.rem(y + d, ny)
            start(y_buf.at[slot, y], y_buf.at[slot, y], y_sem.at[slot], dev_y(k))

        def result():
            wait(y_buf.at[slot, pl.ds(0, ny - 1)], y_sem.at[slot])
            total = y_buf[slot, 0]
            for k in range(1, ny):
                total = total + y_buf[slot, k]
            return total

        return result

    for it in range(ITERS):
        if it > 0:
            scale = jnp.broadcast_to(1.0 / mol_count / row_sum, (8, mols))
            col_pass(other, scale)
        else:
            pl.semaphore_wait(barrier, nx * nz + ny - 1)
        col_vec(other, half_buf.at[it, 0])
        start(half_buf.at[it, 0], half_buf.at[it, 1], half_sem.at[it], twin)
        if it > 0:
            col_pass(core, scale)
        mine = a_buf.at[it, chip]
        col_vec(core, mine)
        wait(half_buf.at[it, 1], half_sem.at[it])
        mine[...] = mine[...] + half_buf[it, 1]
        for p in away:
            start(mine, mine, a_sem.at[it], dev(*chip_at(p), core))
        wait(a_buf.at[it, pl.ds(0, nx * nz - 1)], a_sem.at[it])
        col_mass = jnp.sum(a_buf[it], axis=0)
        cs_buf[it, core] = 1.0 / clu_count / col_mass
        start(cs_buf.at[it, core], cs_buf.at[it, core], cs_sem.at[it], twin)
        spread(core, cs_buf.at[it, core])
        acc = row_pass(core, zero)
        wait(cs_buf.at[it, other], cs_sem.at[it])
        spread(other, cs_buf.at[it, other])
        acc = row_pass(other, acc)
        row_sum = sum_cols(it, jnp.sum(acc, axis=0, keepdims=True))()

    inv = 1.0 / row_sum
    for j in range(mols // 128):
        s = slice(128 * j, 128 * (j + 1))
        hi, lo = split(xu_ref[s, :] * to_sublanes(inv[:, s]))
        xc_ref[s, :] = jnp.concatenate([hi, lo], axis=1)

    size = clus // CHUNKS
    part = size // 2

    class Axis:
        def __init__(self, n, place, at_place):
            self.n, self.place, self.at_place = n, place, at_place

        def peers(self):
            for d in near(self.n):
                to = lax.rem(self.place + d, self.n)
                yield to, self.at_place(to)

    x_axis = Axis(nx, x, lambda k: dev(k, z, core))
    z_axis = Axis(nz, z, lambda k: dev(x, k, core))
    sub = part // (nx * nz)

    def axes(k):
        return (z_axis, x_axis) if k in Z_FIRST else (x_axis, z_axis)

    def row_at(k, core_at, first=0, second=0):
        return k * size + core_at * part + first * (part // axes(k)[0].n) + second * sub

    def sums(r):
        n = r.size
        p = jnp.dot(jnp.concatenate(split(e_ref[r, :]), axis=0), xc_ref[...], preferred_element_type=F32)
        p = p[:, 0:128] + p[:, 128:256]
        return (p[0:n] + p[n:2 * n]) * csb_ref[r, :]

    def to_twin(k):
        return remote(send_buf.at[k, other], core_buf.at[k], core_sem.at[k, 0], core_sem.at[k, 1], twin)

    def scatter(k):
        one = axes(k)[0]
        blk = part // one.n
        to_twin(k).wait_recv()
        send_buf[k, core] = send_buf[k, core] + core_buf[k]
        for to, peer in one.peers():
            start(send_buf.at[k, core, at(to * blk, blk)], xr_buf.at[k, at(one.place * blk, blk)], xr_sem.at[k], peer)
        xr_buf[k, at(one.place * blk, blk), :] = send_buf[k, core, at(one.place * blk, blk), :]

    last = CHUNKS - 1

    def products(i, _):
        k, own = lax.div(i, 2), lax.rem(i, 2)
        which = lax.rem(core + 1 + own, 2)
        send_buf[k, which] = sums(at(row_at(k, which), part))

        @pl.when(own == 0)
        def _():
            to_twin(k).start()

        for done in range(last):
            @pl.when(i == 2 * done + 2)
            def _():
                scatter(done)

        return 0

    lax.fori_loop(0, 2 * CHUNKS, products, 0)
    scatter(last)

    def total_of(ref, n):
        rows = ref.shape[0] // n
        total = ref[0:rows, :]
        for j in range(1, n):
            total = total + ref[j * rows:(j + 1) * rows, :]
        return total

    def after_first(k):
        one, two = axes(k)
        blk = part // one.n
        wait(xr_buf.at[k, pl.ds(0, part - blk)], xr_sem.at[k])
        zs_buf[k, 0:blk, :] = total_of(xr_buf.at[k], one.n)
        for to, peer in two.peers():
            start(zs_buf.at[k, at(to * sub, sub)], zr_buf.at[k, at(two.place * sub, sub)], zr_sem.at[k], peer)
        zr_buf[k, at(two.place * sub, sub), :] = zs_buf[k, at(two.place * sub, sub), :]

    def after_second(k):
        one, two = axes(k)
        blk = part // one.n
        wait(zr_buf.at[k, pl.ds(0, blk - sub)], zr_sem.at[k])
        r = at(row_at(k, core, one.place, two.place), sub)
        out_ref[r, :] = unit_rows(total_of(zr_buf.at[k, pl.ds(0, blk)], two.n))
        if k in ONE_SHOT:
            for p in away:
                start(out_ref.at[r], out_ref.at[r], gx_sem.at[k], dev(*chip_at(p), core))
            return
        for _, peer in two.peers():
            start(out_ref.at[r], out_ref.at[r], gz_sem.at[k], peer)

    def after_gather_second(k):
        one = axes(k)[0]
        blk = part // one.n
        wait(zr_buf.at[k, pl.ds(0, blk - sub)], gz_sem.at[k])
        ref = out_ref.at[at(row_at(k, core, one.place), blk)]
        for _, peer in one.peers():
            start(ref, ref, gx_sem.at[k], peer)

    def after_gather_first(k):
        own = sub if k in ONE_SHOT else part // axes(k)[0].n
        wait(xr_buf.at[k, pl.ds(0, part - own)], gx_sem.at[k])
        ref = out_ref.at[at(row_at(k, core), part)]
        start(ref, ref, gc_sem.at[k], twin)
        leave(k, core).start()

    def leave(k, core_at):
        r = at(row_at(k, core_at), part)
        return pltpu.make_async_copy(out_ref.at[r], out_hbm.at[r], out_sem.at[k, core_at])

    def numer_pass(i, acc):
        for g in range(step_r // 8):
            r = at(i * step_r + g * 8, 8)
            acc = acc + scaled(r) * t_ref[r, :]
        return acc

    pieces = 4
    numer = zero

    def numer_piece(i):
        return lax.fori_loop(2 * steps * i // pieces, 2 * steps * (i + 1) // pieces, numer_pass, numer)

    def end(k):
        wait(core_buf.at[k], gc_sem.at[k])
        leave(k, other).start()

    after_first(0)
    after_first(1)
    numer = numer_piece(0)
    after_first(2)
    numer = numer_piece(1)
    after_first(3)
    numer = numer_piece(2)
    after_second(0)
    numer = numer_piece(3)
    numer = sum_cols(ITERS, jnp.sum(numer, axis=0, keepdims=True))
    after_second(1)
    after_second(2)
    after_second(3)
    after_gather_second(0)
    after_gather_second(1)
    sim_ref[...] = numer() / row_sum * (1.0 / INV_TEMP)
    after_gather_first(0)
    after_gather_first(1)
    end(0)
    after_gather_first(2)
    end(1)
    after_gather_first(3)
    end(2)
    end(3)

    drain()
    for k in range(CHUNKS):
        to_twin(k).wait_send()
        leave(k, 0).wait()
        leave(k, 1).wait()


def hand_out(centres_ref, sim_ref, out_ref, expected_ref, sem):
    rows = out_ref.shape[0] // 4
    copies = [pltpu.make_async_copy(sim_ref, expected_ref, sem.at[4])]
    for i in range(4):
        r = pl.ds(i * rows, rows)
        copies.append(pltpu.make_async_copy(centres_ref.at[r], out_ref.at[r], sem.at[i]))
    for copy in copies:
        copy.start()
    for copy in copies:
        copy.wait()


def local(dims, embeddings, centres):
    nx, nz, ny = dims
    mols, emb = embeddings.shape
    clus = centres.shape[0]
    half = clus // 2
    size = clus // CHUNKS
    part = size // 2
    dma = pltpu.SemaphoreType.DMA
    new_centres, expected = pl.pallas_call(
        functools.partial(kernel, dims, mols * lax.axis_size("rows"), clus * lax.axis_size("cols")),
        out_shape=(jax.ShapeDtypeStruct((clus, emb), F32), jax.ShapeDtypeStruct((1, mols), F32)),
        in_specs=[pl.BlockSpec(memory_space=pl.ANY)] * 2,
        out_specs=(pl.BlockSpec(memory_space=pl.ANY), pl.BlockSpec(memory_space=pltpu.VMEM)),
        scratch_shapes=[
            pltpu.VMEM((clus, emb), F32),
            pltpu.VMEM((clus, mols), F32),
            pltpu.VMEM((clus, mols), F32),
            pltpu.VMEM((clus, 2 * emb), BF16),
            pltpu.VMEM((mols, 2 * emb), BF16),
            pltpu.VMEM((mols, emb), F32),
            pltpu.VMEM((clus, 128), F32),
            pltpu.VMEM((clus, 128), F32),
            pltpu.VMEM((ITERS, 2, half // 128, 128), F32),
            pltpu.VMEM((ITERS, nx * nz, half // 128, 128), F32),
            pltpu.VMEM((ITERS, 2, half // 128, 128), F32),
            pltpu.VMEM((ITERS + 1, ny, 1, mols), F32),
            pltpu.VMEM((CHUNKS, part, emb), F32),
            pltpu.VMEM((CHUNKS, 2, part, emb), F32),
            pltpu.VMEM((CHUNKS, part, emb), F32),
            pltpu.VMEM((CHUNKS, part // min(nx, nz), emb), F32),
            pltpu.VMEM((CHUNKS, part // min(nx, nz), emb), F32),
            dma((mols // min(256, mols), 2)),
            dma((CHUNKS, 2)),
            dma((ITERS, 2)),
            dma((ITERS, 2)),
            dma((ITERS, 2)),
            dma((ITERS + 1, 2)),
            dma((CHUNKS, 2)),
            dma((CHUNKS, 2)),
            dma((CHUNKS, 2)),
            dma((CHUNKS, 2)),
            dma((CHUNKS, 2)),
            dma((CHUNKS, 2)),
        ],
        compiler_params=pltpu.CompilerParams(
            collective_id=0, has_side_effects=True, vmem_limit_bytes=62 * 1024 * 1024),
        cost_estimate=pl.CostEstimate(flops=2 * 8 * mols * clus * emb, bytes_accessed=4 * 1024 * 1024,
                                      transcendentals=mols * clus),
    )(embeddings, centres)
    new_centres, expected = pl.pallas_call(
        hand_out,
        out_shape=(jax.ShapeDtypeStruct((clus, emb), F32), jax.ShapeDtypeStruct((1, mols), F32)),
        in_specs=[pl.BlockSpec(memory_space=pltpu.VMEM)] * 2,
        out_specs=(pl.BlockSpec(memory_space=pl.ANY),) * 2,
        scratch_shapes=[dma((5,))],
    )(new_centres, expected)
    return new_centres, expected.reshape(mols)


def solution(mesh, dims=(CHIPS_X, CHIPS_Z, CHIPS_Y)):
    return jax.shard_map(
        functools.partial(local, dims), mesh=mesh, in_specs=(P("rows", None), P("cols", None)),
        out_specs=(P("cols", None), P("rows")), check_vma=False)
```
